256 devices in a mesh: clip: 8 (over x, core), frame: 32 (over y, z).
Axes of the slice: x: 4, y: 4, z: 8, core: 2. Of those that a mesh axis runs over, the one named last changes fastest.
Arguments:
- queries: bfloat16 [65536, 1024], P(('clip', 'frame')), may hold values from -216 to 216
- keys: bfloat16 [65536, 1024], P(('clip', 'frame')), may hold values from -6 to 6
- values: bfloat16 [65536, 1024], P(('clip', 'frame')), may hold values from -6 to 6
- cotangent: bfloat16 [65536, 1024], P(('clip', 'frame')), may hold values from -6 to 6
- partners: int32 [256, 6], P(('clip', 'frame')), may hold values from 0 to 255, as said below
- counts: int32 [256], P(('clip', 'frame')), may hold values from 1 to 6, as said below
Outputs:
- attended: bfloat16 [65536, 1024], P(('clip', 'frame'))
- query_grad: bfloat16 [65536, 1024], P(('clip', 'frame'))
- key_grad: bfloat16 [65536, 1024], P(('clip', 'frame'))
- value_grad: bfloat16 [65536, 1024], P(('clip', 'frame'))
The draws below stay inside these ranges and needn't reach their ends.
Inputs may be any that keep to these rules, and one draw needn't show every extreme that they name: `partners`: row g lists distinct frames other than g, each either in g's clip group at most 2 positions away from g, or at g's position in the next or the previous clip group (cyclically). Entries past counts[g] are other frame ids. `counts`: some frame has all 6 entries live.
All inputs are finite; a program needn't handle non-finite values.
Results may differ from the reference program's by a relative error of at most 0.035.
Values may be sent and summed in bfloat16 or wider, within the bound.
A program may use at most 128 MiB of HBM per device.

```python
import math
import jax
import jax.numpy as jnp
from jax import lax

HEADS = 16
HEAD_DIM = 64
D = 1024
TOK = 256
REACH = 2
SLOTS = 6
ROWS = 65536
N_CLIP = 8
N_FRAME = 32


def shared_normal(key):
    return jnp.clip(jax.random.normal(key, (N_CLIP * N_FRAME * TOK, HEADS * HEAD_DIM), jnp.float32), -6.0, 6.0)


def draw_keys(key, part):
    common = shared_normal(key)
    return common.astype(jnp.bfloat16)


def draw_queries(key, part):
    common = shared_normal(key)
    key = jax.random.fold_in(key, 5)
    result = 2.0 * jnp.clip(jax.random.normal(key, common.shape, jnp.float32), -6.0, 6.0)
    return result.astype(jnp.bfloat16)


def covisible(key):
    frames = N_CLIP * N_FRAME
    key_order, key_count, key_heavy, key_chosen = jax.random.split(jax.random.fold_in(key, 7), 4)
    index = jnp.arange(frames, dtype=jnp.int32)
    clip_of = index // N_FRAME
    place = index % N_FRAME
    near_steps = jnp.array([o for o in range(-REACH, REACH + 1) if o != 0], jnp.int32)
    near_ids = index[:, None] + near_steps[None, :]
    near_place = place[:, None] + near_steps[None, :]
    near_usable = (near_place >= 0) & (near_place < N_FRAME)
    pass_ids = jnp.stack([(clip_of + 1) % N_CLIP * N_FRAME + place, (clip_of + N_CLIP - 1) % N_CLIP * N_FRAME + place], axis=1)
    candidates = jnp.mod(jnp.concatenate([near_ids, pass_ids], axis=1), frames)
    usable = jnp.concatenate([near_usable, jnp.ones((frames, 2), dtype=bool)], axis=1)
    column = jnp.arange(SLOTS, dtype=jnp.int32)[None, :]
    favour = jnp.where(column < 2 * REACH, 2 ** 20, 0)
    drawn = jax.random.randint(key_order, (frames, SLOTS), 0, 2 ** 20)
    ranking = jnp.where(usable, (drawn + favour) * 16 + column, -1 - column)
    ordering = jnp.argsort(-ranking, axis=1)
    partners = jnp.take_along_axis(candidates, ordering, axis=1).astype(jnp.int32)
    usable_count = jnp.sum(usable.astype(jnp.int32), axis=1)
    typical = jax.random.randint(key_count, (frames,), 1, 5)
    heavy = jax.random.randint(key_heavy, (frames,), 0, 4) == 0
    live_counts = jnp.where(heavy, usable_count, jnp.minimum(typical, usable_count))
    chosen_draw = jax.random.randint(key_chosen, (), 0, frames)
    chosen_frame = chosen_draw // N_FRAME * N_FRAME + REACH + chosen_draw % (N_FRAME - 2 * REACH)
    live_counts = jnp.where(index == chosen_frame, SLOTS, live_counts).astype(jnp.int32)
    return (partners, live_counts)


def draw_partners(key, part):
    return covisible(key)[0]


def draw_counts(key, part):
    return covisible(key)[1]


def steps_of(rng, dims, cuts, least, largest):
    gain, own = 1.0, jax.random.fold_in(rng, 6)
    for dim, parts in cuts:
        heights = jnp.exp(jax.random.uniform(jax.random.fold_in(own, dim), (parts,), jnp.float32, least / len(cuts), largest / len(cuts)))
        gain = gain * jnp.repeat(heights, dims[dim] // parts).reshape([-1 if axis == dim else 1 for axis in range(len(dims))])
    return gain


def noise(rng, dims, deviation, reach, cuts=(), kind=jnp.bfloat16):
    values = jax.random.normal(rng, dims, jnp.float32) * deviation
    if len(cuts) > 0:
        values = steps_of(rng, dims, cuts, -0.22, 0.18) * values
    return jnp.clip(values, min=-reach, max=reach).astype(kind)


def setup_inputs(seed: int = 0) -> dict:
    streams_of = jax.random.split(jax.random.key(seed), 7)
    queries = draw_queries(jax.random.fold_in(streams_of[6], 71), 0)
    keys = draw_keys(jax.random.fold_in(streams_of[6], 71), 0)
    values = noise(streams_of[2], (ROWS, D), 1.0, 6.0, ((0, 256),))
    cotangent = noise(streams_of[3], (ROWS, D), 1.0, 6.0, ((0, 256),))
    partners = draw_partners(jax.random.fold_in(streams_of[6], 71), 0)
    counts = draw_counts(jax.random.fold_in(streams_of[6], 71), 0)
    return dict(queries=queries, keys=keys, values=values, cotangent=cotangent, partners=partners, counts=counts)


def reference(queries, keys, values, cotangent, partners, counts):
    frames = N_CLIP * N_FRAME
    scaling = 1.0 / math.sqrt(HEAD_DIM)
    shaped = (frames, TOK, HEADS, HEAD_DIM)
    query_all = queries.reshape(shaped)
    key_all = keys.reshape(shaped)
    value_all = values.reshape(shaped)
    grad_all = cotangent.reshape(shaped)
    own_ids = jnp.arange(frames, dtype=jnp.int32)[:, None]
    key_ids = jnp.concatenate([own_ids, partners.astype(jnp.int32)], axis=1)
    slot_live = jnp.concatenate([jnp.ones((frames, 1), dtype=bool), jnp.arange(SLOTS, dtype=jnp.int32)[None, :] < counts[:, None]], axis=1)

    def one_frame(running, index):
        key_total, value_total = running
        chosen = key_ids[index]
        live = slot_live[index][None, None, :, None]
        live_rows = slot_live[index][:, None, None, None]
        query_f = query_all[index].astype(jnp.float32)
        grad_f = grad_all[index].astype(jnp.float32)
        key_f = key_all[chosen].astype(jnp.float32)
        value_f = value_all[chosen].astype(jnp.float32)
        scores = jnp.einsum('qhe,jkhe->hqjk', query_f, key_f) * scaling
        masked = jnp.where(live, scores, -jnp.inf)
        top = lax.optimization_barrier(jnp.max(masked, axis=(2, 3)))
        total = lax.optimization_barrier(jnp.sum(jnp.exp(masked - top[:, :, None, None]), axis=(2, 3)))
        log_total = top + jnp.log(total)
        weights = jnp.where(live, jnp.exp(scores - log_total[:, :, None, None]), 0.0)
        weights_low = lax.optimization_barrier(weights.astype(jnp.bfloat16)).astype(jnp.float32)
        attended = jnp.einsum('hqjk,jkhe->qhe', weights_low, value_f).astype(jnp.bfloat16)
        attended_f = lax.optimization_barrier(attended).astype(jnp.float32)
        spread = lax.optimization_barrier(jnp.sum(grad_f * attended_f, axis=2)).T
        weight_grad = jnp.einsum('qhe,jkhe->hqjk', grad_f, value_f)
        score_grad = (weights * (weight_grad - spread[:, :, None, None])).astype(jnp.bfloat16)
        score_grad = lax.optimization_barrier(score_grad).astype(jnp.float32)
        query_grad = (jnp.einsum('hqjk,jkhe->qhe', score_grad, key_f) * scaling).astype(jnp.bfloat16)
        key_part = (jnp.einsum('hqjk,qhe->jkhe', score_grad, query_f) * scaling).astype(jnp.bfloat16)
        value_part = jnp.einsum('hqjk,qhe->jkhe', weights_low, grad_f).astype(jnp.bfloat16)
        key_part = lax.optimization_barrier(key_part).astype(jnp.float32)
        value_part = lax.optimization_barrier(value_part).astype(jnp.float32)
        key_part = jnp.where(live_rows, key_part, 0.0)
        value_part = jnp.where(live_rows, value_part, 0.0)
        key_total = key_total.at[chosen].add(key_part)
        value_total = value_total.at[chosen].add(value_part)
        return ((key_total, value_total), (attended, query_grad))
    start = (jnp.zeros(shaped, jnp.float32), jnp.zeros(shaped, jnp.float32))
    totals, outputs = lax.scan(one_frame, start, jnp.arange(frames, dtype=jnp.int32))
    flat = (frames * TOK, HEADS * HEAD_DIM)
    return (outputs[0].reshape(flat), outputs[1].reshape(flat), totals[0].astype(jnp.bfloat16).reshape(flat), totals[1].astype(jnp.bfloat16).reshape(flat))
```

```python
import functools
import math

import jax
import jax.numpy as jnp
from jax import lax
from jax.experimental import pallas as pl
from jax.experimental.pallas import tpu as pltpu
from jax.sharding import PartitionSpec as P

HEADS = 16
HEAD_DIM = 64
TOK = 256
WIDTH = 1024
SLOTS = 6
PAIR = 2 * HEAD_DIM
PAIRS = WIDTH // PAIR
SCALE = 1.0 / math.sqrt(HEAD_DIM)
FAR = 3e38
LAG = 3
MESH = pl.DeviceIdType.MESH

OWN = 6
FRAMES = 7


def kernel(
    partners, counts, q_hbm, k_hbm, v_hbm, g_hbm,
    att_hbm, dq_hbm, dk_hbm, dv_hbm,
    kv, tout, tin, pb, ds, q_in, g_in, qm, qt, gm, gt, o_t, dq_t, att_out, dq_out,
    mst, lst, cst, bias,
    in_sem, out_sem, kv_send, kv_recv, t_send, t_recv,
):
    c = lax.axis_index("clip")
    f = lax.axis_index("frame")
    clips = lax.axis_size("clip")
    frames = lax.axis_size("frame")
    right, left = (c, f + 1), (c, f - 1)
    up = (lax.rem(c + 1, clips), f)
    down = (lax.rem(c + clips - 1, clips), f)
    has_r, has_l = f < frames - 1, f > 0
    has_rr, has_ll = f < frames - 2, f > 1
    has_both = has_r & has_l

    def columns(p):
        return pl.ds(pl.multiple_of(p * PAIR, PAIR), PAIR)

    def fetch(i, p):
        src = (k_hbm, v_hbm, q_hbm, g_hbm)[i]
        dst = kv.at[OWN, p, i] if i < 2 else (q_in, g_in)[i - 2].at[p]
        return pltpu.make_async_copy(src.at[:, columns(p)], dst, in_sem.at[i, p])

    def store(i, p):
        src = (att_out, dq_out)[i].at[p] if i < 2 else tout.at[OWN, p, i - 2]
        dst = (att_hbm, dq_hbm, dk_hbm, dv_hbm)[i]
        return pltpu.make_async_copy(src, dst.at[:, columns(p)], out_sem.at[i, p])

    def remote(src, dst, send, recv, device):
        return pltpu.make_async_remote_copy(
            src_ref=src, dst_ref=dst, send_sem=send, recv_sem=recv, device_id=device, device_id_type=MESH
        )

    kv_routes = [
        (OWN, 5, right, has_r, has_l),
        (OWN, 4, left, has_l, has_r),
        (OWN, 3, up, None, None),
        (OWN, 2, down, None, None),
        (5, 1, right, has_both, has_ll),
        (4, 0, left, has_both, has_rr),
    ]

    def kv_copy(i, p):
        here, there, device, _, _ = kv_routes[i]
        return remote(kv.at[here, p], kv.at[there, p], kv_send.at[i, p], kv_recv.at[there, p], device)

    t_routes = [
        (0, 0, right, has_rr, has_both),
        (1, 1, left, has_ll, has_both),
        (2, 3, up, None, None),
        (3, 2, down, None, None),
        (4, 5, right, has_r, has_l),
        (5, 4, left, has_l, has_r),
    ]

    def t_copy(i, p):
        slot, there, device, _, _ = t_routes[i]
        return remote(tout.at[slot, p], tin.at[there, p], t_send.at[i, p], t_recv.at[there, p], device)

    def when(condition, action):
        if condition is None:
            action()
        else:
            pl.when(condition)(action)

    def start(copy, routes, i, p):
        when(routes[i][3], lambda: copy(i, p).start())

    def wait_send(copy, routes, i, p):
        when(routes[i][3], lambda: copy(i, p).wait_send())

    def wait_recv(copy, routes, i, p):
        when(routes[i][4], lambda: copy(i, p).wait_recv())

    def each_pair(body):
        def step(p, carry):
            body(p)
            return carry

        lax.fori_loop(0, PAIRS, step, 0)

    @each_pair
    def _(p):
        for i in range(4):
            fetch(i, p).start()

    barrier = pltpu.get_barrier_semaphore()
    for device, present in ((right, has_r), (left, has_l), (up, None), (down, None)):
        when(
            present,
            functools.partial(pl.semaphore_signal, barrier, inc=1, device_id=device, device_id_type=MESH),
        )
    pl.semaphore_wait(barrier, 2 + has_r.astype(jnp.int32) + has_l.astype(jnp.int32))

    @each_pair
    def _(p):
        for i in (0, 1):
            fetch(i, p).wait()
        for i in range(4):
            start(kv_copy, kv_routes, i, p)

    live = counts[0]
    me = c * frames + f
    targets = [
        (me + 2, has_rr),
        (me - 2, has_ll),
        (up[0] * frames + f, None),
        (down[0] * frames + f, None),
        (me + 1, has_r),
        (me - 1, has_l),
    ]
    for slot, (target, present) in enumerate(targets):
        found = jnp.int32(0)
        for s in range(SLOTS):
            found = found + jnp.where((partners[0, s] == target) & (s < live), 1, 0)
        if present is not None:
            found = jnp.where(present, found, 0)
        bias[slot] = jnp.where(found > 0, 0.0, FAR).astype(jnp.float32)
    bias[OWN] = jnp.float32(0.0)

    for slot, present in ((0, has_rr), (1, has_ll), (4, has_r), (5, has_l)):

        @pl.when(jnp.logical_not(present))
        def _():
            @each_pair
            def _(p):
                kv[slot, p] = jnp.zeros(kv.shape[2:], kv.dtype)

    for slot, present in ((0, has_both), (1, has_both), (4, has_r), (5, has_l)):

        @pl.when(jnp.logical_not(present))
        def _():
            @each_pair
            def _(p):
                tin[slot, p] = jnp.zeros(tin.shape[2:], tin.dtype)

    @each_pair
    def _(p):
        for i in (2, 3):
            fetch(i, p).wait()
        lane = lax.broadcasted_iota(jnp.int32, (TOK, PAIR), 1)
        row = lax.broadcasted_iota(jnp.int32, (PAIR, TOK), 0)
        q = q_in[p].astype(jnp.float32) * SCALE
        g = g_in[p].astype(jnp.float32)
        q_turned, g_turned = q.T, g.T
        for h in range(2):
            mine = (lane < HEAD_DIM) if h == 0 else (lane >= HEAD_DIM)
            mine_t = (row < HEAD_DIM) if h == 0 else (row >= HEAD_DIM)
            rows = pl.ds(h * TOK, TOK)
            qm[p, rows, :] = jnp.where(mine, q, 0.0).astype(jnp.bfloat16)
            gm[p, rows, :] = jnp.where(mine, g, 0.0).astype(jnp.bfloat16)
            qt[p, h] = jnp.where(mine_t, q_turned, 0.0).astype(jnp.bfloat16)
            gt[p, h] = jnp.where(mine_t, g_turned, 0.0).astype(jnp.bfloat16)

    def weigh(p, j):
        shift = bias[j]
        for h in range(2):
            cols = pl.ds(h * TOK, TOK)
            s = jnp.dot(kv[j, p, 0], qt[p, h], preferred_element_type=jnp.float32)
            top = jnp.max(s, axis=0, keepdims=True)
            e = jnp.exp(s - (top + shift))
            mst[p, j, :, cols] = top - shift
            lst[p, j, :, cols] = jnp.sum(e, axis=0, keepdims=True)
            pb[p, j, :, cols] = e.astype(jnp.bfloat16)

    def weigh_slots(p, first, last):
        def step(j, carry):
            weigh(p, j)
            return carry

        lax.fori_loop(first, last, step, 0)

    @each_pair
    def _(p):
        for i in (0, 1):
            wait_recv(kv_copy, kv_routes, i, p)
            start(kv_copy, kv_routes, 4 + i, p)
        for i in (2, 3):
            wait_recv(kv_copy, kv_routes, i, p)
        weigh_slots(p, 2, FRAMES)

    def near_terms(p):
        for i in (0, 1):
            wait_recv(t_copy, t_routes, i, p)
            total = tout[4 + i, p].astype(jnp.float32) + tin[i, p].astype(jnp.float32)
            tout[4 + i, p] = total.astype(jnp.bfloat16)
            start(t_copy, t_routes, 4 + i, p)

    @each_pair
    def _(p):
        for i in (4, 5):
            wait_recv(kv_copy, kv_routes, i, p)
        weigh_slots(p, 0, 2)

        top = jnp.max(mst[p], axis=0)
        total = jnp.zeros((1, 2 * TOK), jnp.float32)
        for j in range(FRAMES):
            e = jnp.exp(mst[p, j] - top)
            cst[j] = e
            total = total + e * lst[p, j]
        inverse = 1.0 / total
        for j in range(FRAMES):
            cst[j] = cst[j] * inverse

        o_t[...] = jnp.zeros_like(o_t)
        dq_t[...] = jnp.zeros_like(dq_t)

        def mix(j, carry):
            v_turned = kv[j, p, 1].T
            for h in range(2):
                cols = pl.ds(h * TOK, TOK)
                rows = slice(h * HEAD_DIM, (h + 1) * HEAD_DIM)
                part = jnp.dot(v_turned[rows], pb[p, j, :, cols], preferred_element_type=jnp.float32)
                o_t[rows] += part * cst[j, :, cols]
            return carry

        lax.fori_loop(0, FRAMES, mix, 0)
        attended = o_t[...].astype(jnp.bfloat16)
        attended_f = attended.astype(jnp.float32)
        att_out[p] = attended_f.T.astype(jnp.bfloat16)
        spread = [jnp.sum(gt[p, h].astype(jnp.float32) * attended_f, axis=0, keepdims=True) for h in range(2)]

        def grads(j, carry):
            k_turned = kv[j, p, 0].T
            for h in range(2):
                cols = pl.ds(h * TOK, TOK)
                rows = slice(h * HEAD_DIM, (h + 1) * HEAD_DIM)
                w = pb[p, j, :, cols].astype(jnp.float32) * cst[j, :, cols]
                pb[p, j, :, cols] = w.astype(jnp.bfloat16)
                dw = jnp.dot(kv[j, p, 1], gt[p, h], preferred_element_type=jnp.float32)
                d = (w * (dw - spread[h])).astype(jnp.bfloat16)
                ds[:, cols] = d
                dq_t[rows] += jnp.dot(k_turned[rows], d, preferred_element_type=jnp.float32)
            tout[j, p, 0] = jnp.dot(ds[...], qm[p], preferred_element_type=jnp.float32).astype(jnp.bfloat16)
            tout[j, p, 1] = jnp.dot(pb[p, j], gm[p], preferred_element_type=jnp.float32).astype(jnp.bfloat16)

            for after, sent in ((1, (0, 1)), (3, (2, 3))):

                @pl.when(j == after)
                def _():
                    for i in sent:
                        start(t_copy, t_routes, i, p)

            return carry

        lax.fori_loop(0, FRAMES, grads, 0)
        dq_out[p] = (dq_t[...] * SCALE).T.astype(jnp.bfloat16)
        for i in (0, 1):
            store(i, p).start()

        @pl.when(p >= LAG)
        def _():
            near_terms(p - LAG)

    def flush(p, carry):
        near_terms(p)
        return carry

    lax.fori_loop(PAIRS - LAG, PAIRS, flush, 0)

    @each_pair
    def _(p):
        for i in range(2, 6):
            wait_recv(t_copy, t_routes, i, p)
        total = tout[OWN, p].astype(jnp.float32)
        for i in range(2, 6):
            total = total + tin[i, p].astype(jnp.float32)
        tout[OWN, p] = total.astype(jnp.bfloat16)
        for i in (2, 3):
            store(i, p).start()

    @each_pair
    def _(p):
        for i in range(6):
            wait_send(kv_copy, kv_routes, i, p)
            wait_send(t_copy, t_routes, i, p)
        for i in range(4):
            store(i, p).wait()


def shards(queries, keys, values, cotangent, partners, counts):
    block = jax.ShapeDtypeStruct((TOK, WIDTH), jnp.bfloat16)
    smem = pl.BlockSpec(memory_space=pltpu.SMEM)
    whole = pl.BlockSpec(memory_space=pl.ANY)
    low = jnp.bfloat16
    return pl.pallas_call(
        kernel,
        out_shape=(block,) * 4,
        in_specs=[smem, smem] + [whole] * 4,
        out_specs=(whole,) * 4,
        scratch_shapes=[
            pltpu.VMEM((FRAMES, PAIRS, 2, TOK, PAIR), low),
            pltpu.VMEM((FRAMES, PAIRS, 2, TOK, PAIR), low),
            pltpu.VMEM((6, PAIRS, 2, TOK, PAIR), low),
            pltpu.VMEM((PAIRS, FRAMES, TOK, 2 * TOK), low),
            pltpu.VMEM((TOK, 2 * TOK), low),
            pltpu.VMEM((PAIRS, TOK, PAIR), low),
            pltpu.VMEM((PAIRS, TOK, PAIR), low),
            pltpu.VMEM((PAIRS, 2 * TOK, PAIR), low),
            pltpu.VMEM((PAIRS, 2, PAIR, TOK), low),
            pltpu.VMEM((PAIRS, 2 * TOK, PAIR), low),
            pltpu.VMEM((PAIRS, 2, PAIR, TOK), low),
            pltpu.VMEM((PAIR, TOK), jnp.float32),
            pltpu.VMEM((PAIR, TOK), jnp.float32),
            pltpu.VMEM((PAIRS, TOK, PAIR), low),
            pltpu.VMEM((PAIRS, TOK, PAIR), low),
            pltpu.VMEM((PAIRS, FRAMES, 1, 2 * TOK), jnp.float32),
            pltpu.VMEM((PAIRS, FRAMES, 1, 2 * TOK), jnp.float32),
            pltpu.VMEM((FRAMES, 1, 2 * TOK), jnp.float32),
            pltpu.SMEM((FRAMES,), jnp.float32),
            pltpu.SemaphoreType.DMA((4, PAIRS)),
            pltpu.SemaphoreType.DMA((4, PAIRS)),
            pltpu.SemaphoreType.DMA((6, PAIRS)),
            pltpu.SemaphoreType.DMA((6, PAIRS)),
            pltpu.SemaphoreType.DMA((6, PAIRS)),
            pltpu.SemaphoreType.DMA((6, PAIRS)),
        ],
        compiler_params=pltpu.CompilerParams(
            collective_id=0, has_side_effects=True, vmem_limit_bytes=60 * 2**20
        ),
    )(partners, counts, queries, keys, values, cotangent)


def solution(mesh):
    rows = P(("clip", "frame"), None)
    return jax.shard_map(
        shards,
        mesh=mesh,
        in_specs=(rows, rows, rows, rows, rows, P(("clip", "frame"))),
        out_specs=(rows, rows, rows, rows),
        check_vma=False,
    )
```

```python
import functools
import math

import jax
import jax.numpy as jnp
from jax import lax
from jax.experimental import pallas as pl
from jax.experimental.pallas import tpu as pltpu
from jax.sharding import PartitionSpec as P

HEADS = 16
HEAD_DIM = 64
TOK = 256
WIDTH = 1024
SLOTS = 6
PAIR = 2 * HEAD_DIM
PAIRS = WIDTH // PAIR
SCALE = 1.0 / math.sqrt(HEAD_DIM)
FAR = 3e38
LAG = 3
MESH = pl.DeviceIdType.MESH

OWN = 6
FRAMES = 7
EARLY = (6, 2, 3, 4, 5)


def kernel(
    partners_hbm, counts_hbm, q_hbm, k_hbm, v_hbm, g_hbm,
    att_hbm, dq_hbm, dk_hbm, dv_hbm,
    kv, tout, tin, pb, q_in, g_in, qm, qt, gm, gt, o_t, att_out, dq_out,
    mst, lst, bias, partners, counts, list_sem,
    in_sem, out_sem, kv_send, kv_recv, t_send, t_recv,
):
    c = lax.axis_index("clip")
    f = lax.axis_index("frame")
    clips = lax.axis_size("clip")
    frames = lax.axis_size("frame")
    right, left = (c, f + 1), (c, f - 1)
    up = (lax.rem(c + 1, clips), f)
    down = (lax.rem(c + clips - 1, clips), f)
    has_r, has_l = f < frames - 1, f > 0
    has_rr, has_ll = f < frames - 2, f > 1
    has_both = has_r & has_l

    def columns(p):
        return pl.ds(pl.multiple_of(p * PAIR, PAIR), PAIR)

    def fetch(i, p):
        src = (k_hbm, v_hbm, q_hbm, g_hbm)[i]
        dst = kv.at[OWN, p, i] if i < 2 else (q_in, g_in)[i - 2].at[p]
        return pltpu.make_async_copy(src.at[:, columns(p)], dst, in_sem.at[i, p])

    def store(i, p):
        src = (att_out, dq_out)[i].at[p] if i < 2 else tout.at[OWN, p, i - 2]
        dst = (att_hbm, dq_hbm, dk_hbm, dv_hbm)[i]
        return pltpu.make_async_copy(src, dst.at[:, columns(p)], out_sem.at[i, p])

    def remote(src, dst, send, recv, device):
        return pltpu.make_async_remote_copy(
            src_ref=src, dst_ref=dst, send_sem=send, recv_sem=recv, device_id=device, device_id_type=MESH
        )

    kv_routes = [
        (OWN, 5, right, has_r, has_l),
        (OWN, 4, left, has_l, has_r),
        (OWN, 3, up, None, None),
        (OWN, 2, down, None, None),
        (5, 1, right, has_both, has_ll),
        (4, 0, left, has_both, has_rr),
    ]

    def kv_copy(i, p):
        here, there, device, _, _ = kv_routes[i]
        return remote(kv.at[here, p], kv.at[there, p], kv_send.at[i, p], kv_recv.at[there, p], device)

    t_routes = [
        (0, 0, right, has_rr, has_both),
        (1, 1, left, has_ll, has_both),
        (2, 3, up, None, None),
        (3, 2, down, None, None),
        (4, 5, right, has_r, has_l),
        (5, 4, left, has_l, has_r),
    ]

    def t_copy(i, p):
        slot, there, device, _, _ = t_routes[i]
        return remote(tout.at[slot, p], tin.at[there, p], t_send.at[i, p], t_recv.at[there, p], device)

    def when(condition, action):
        if condition is None:
            action()
        else:
            pl.when(condition)(action)

    def start(copy, routes, i, p):
        when(routes[i][3], lambda: copy(i, p).start())

    def wait_send(copy, routes, i, p):
        when(routes[i][3], lambda: copy(i, p).wait_send())

    def wait_recv(copy, routes, i, p):
        when(routes[i][4], lambda: copy(i, p).wait_recv())

    def each_pair(body):
        def step(p, carry):
            body(p)
            return carry

        lax.fori_loop(0, PAIRS, step, 0)

    lists = [
        pltpu.make_async_copy(partners_hbm, partners, list_sem.at[0]),
        pltpu.make_async_copy(counts_hbm, counts, list_sem.at[1]),
    ]
    for copy in lists:
        copy.start()

    @each_pair
    def _(p):
        for i in range(4):
            fetch(i, p).start()

    barrier = pltpu.get_barrier_semaphore()
    for device, present in ((right, has_r), (left, has_l), (up, None), (down, None)):
        when(
            present,
            functools.partial(pl.semaphore_signal, barrier, inc=1, device_id=device, device_id_type=MESH),
        )
    pl.semaphore_wait(barrier, 2 + has_r.astype(jnp.int32) + has_l.astype(jnp.int32))

    @each_pair
    def _(p):
        for i in (0, 1):
            fetch(i, p).wait()
        for i in range(4):
            start(kv_copy, kv_routes, i, p)

    for copy in lists:
        copy.wait()
    live = counts[0]
    me = c * frames + f
    targets = [
        (me + 2, has_rr),
        (me - 2, has_ll),
        (up[0] * frames + f, None),
        (down[0] * frames + f, None),
        (me + 1, has_r),
        (me - 1, has_l),
    ]
    for slot, (target, present) in enumerate(targets):
        found = jnp.int32(0)
        for s in range(SLOTS):
            found = found + jnp.where((partners[0, s] == target) & (s < live), 1, 0)
        if present is not None:
            found = jnp.where(present, found, 0)
        bias[slot] = jnp.where(found > 0, 0.0, FAR).astype(jnp.float32)
    bias[OWN] = jnp.float32(0.0)

    for slot, present in ((0, has_rr), (1, has_ll), (4, has_r), (5, has_l)):

        @pl.when(jnp.logical_not(present))
        def _():
            @each_pair
            def _(p):
                kv[slot, p] = jnp.zeros(kv.shape[2:], kv.dtype)

    for slot, present in ((0, has_both), (1, has_both), (4, has_r), (5, has_l)):

        @pl.when(jnp.logical_not(present))
        def _():
            @each_pair
            def _(p):
                tin[slot, p] = jnp.zeros(tin.shape[2:], tin.dtype)

    @each_pair
    def _(p):
        for i in (2, 3):
            fetch(i, p).wait()
        lane = lax.broadcasted_iota(jnp.int32, (TOK, PAIR), 1)
        row = lax.broadcasted_iota(jnp.int32, (PAIR, TOK), 0)
        q = q_in[p].astype(jnp.float32) * SCALE
        g = g_in[p].astype(jnp.float32)
        q_turned, g_turned = q.T, g.T
        for h in range(2):
            mine = (lane < HEAD_DIM) if h == 0 else (lane >= HEAD_DIM)
            mine_t = (row < HEAD_DIM) if h == 0 else (row >= HEAD_DIM)
            rows = pl.ds(h * TOK, TOK)
            qm[p, rows, :] = jnp.where(mine, q, 0.0).astype(jnp.bfloat16)
            gm[p, rows, :] = jnp.where(mine, g, 0.0).astype(jnp.bfloat16)
            qt[p, h] = jnp.where(mine_t, q_turned, 0.0).astype(jnp.bfloat16)
            gt[p, h] = jnp.where(mine_t, g_turned, 0.0).astype(jnp.bfloat16)

    halves = [slice(h * HEAD_DIM, (h + 1) * HEAD_DIM) for h in range(2)]
    both = [slice(h * TOK, (h + 1) * TOK) for h in range(2)]

    def mul(a, b):
        return jnp.dot(a, b, preferred_element_type=jnp.float32)

    def weigh(p, slots):
        def front(j):
            return [mul(kv[j, p, 0], qt[p, h]) for h in range(2)]

        def middle(j, scores):
            tops, sums = [], []
            for h in range(2):
                top = jnp.max(scores[h], axis=0, keepdims=True)
                e = jnp.exp(scores[h] - (top + bias[j]))
                tops.append(top - bias[j])
                sums.append(jnp.sum(e, axis=0, keepdims=True))
                pb[p, j, :, both[h]] = e.astype(jnp.bfloat16)
            return jnp.concatenate(tops, axis=1), jnp.concatenate(sums, axis=1)

        def back(j):
            v_turned = kv[j, p, 1].T
            return [mul(v_turned[halves[h]], pb[p, j, :, both[h]]) for h in range(2)]

        coming = front(slots[0])
        tops, sums, parts = [], [], []
        for n, j in enumerate(slots):
            scores = coming
            if n + 1 < len(slots):
                coming = front(slots[n + 1])
            if n > 0:
                parts.append(back(slots[n - 1]))
            top, total = middle(j, scores)
            tops.append(top)
            sums.append(total)
        parts.append(back(slots[-1]))
        return tops, sums, parts

    @each_pair
    def _(p):
        for i in (0, 1):
            wait_recv(kv_copy, kv_routes, i, p)
            start(kv_copy, kv_routes, 4 + i, p)
        for i in (2, 3):
            wait_recv(kv_copy, kv_routes, i, p)
        tops, sums, parts = weigh(p, EARLY)
        top = functools.reduce(jnp.maximum, tops)
        total = jnp.zeros_like(top)
        mixed = [jnp.zeros((HEAD_DIM, TOK), jnp.float32) for _ in range(2)]
        for n, j in enumerate(EARLY):
            e = jnp.exp(tops[n] - top)
            mst[p, j] = tops[n]
            total = total + e * sums[n]
            mixed = [mixed[h] + parts[n][h] * e[:, both[h]] for h in range(2)]
        mst[p, FRAMES] = top
        lst[p] = total
        for h in range(2):
            o_t[p, halves[h]] = mixed[h]

    def near_terms(p):
        for i in (0, 1):
            wait_recv(t_copy, t_routes, i, p)
            total = tout[4 + i, p].astype(jnp.float32) + tin[i, p].astype(jnp.float32)
            tout[4 + i, p] = total.astype(jnp.bfloat16)
            start(t_copy, t_routes, 4 + i, p)

    @each_pair
    def _(p):
        for i in (4, 5):
            wait_recv(kv_copy, kv_routes, i, p)
        tops, sums, parts = weigh(p, (0, 1))
        tops = tops + [mst[p, j] for j in range(2, FRAMES)]
        early = mst[p, FRAMES]
        top = functools.reduce(jnp.maximum, [tops[0], tops[1], early])
        factors = [jnp.exp(t - top) for t in tops]
        early = jnp.exp(early - top)
        inverse = 1.0 / (early * lst[p] + factors[0] * sums[0] + factors[1] * sums[1])
        factors = [e * inverse for e in factors]
        early = early * inverse

        g_turned = gt[p, 0] + gt[p, 1]
        spread, attended = [], []
        for h in range(2):
            total = o_t[p, halves[h]] * early[:, both[h]]
            for j in (0, 1):
                total = total + parts[j][h] * factors[j][:, both[h]]
            total = total.astype(jnp.bfloat16).astype(jnp.float32)
            attended.append(total)
            spread.append(jnp.sum(g_turned[halves[h]].astype(jnp.float32) * total, axis=0, keepdims=True))
        att_out[p] = jnp.concatenate(attended, axis=0).T.astype(jnp.bfloat16)

        dq_parts = [jnp.zeros((HEAD_DIM, TOK), jnp.float32) for _ in range(2)]

        def front(j):
            return [mul(kv[j, p, 1], gt[p, h]) for h in range(2)]

        def middle(j, dws):
            ws, dss = [], []
            for h in range(2):
                w = pb[p, j, :, both[h]].astype(jnp.float32) * factors[j][:, both[h]]
                ws.append(w.astype(jnp.bfloat16))
                dss.append((w * (dws[h] - spread[h])).astype(jnp.bfloat16))
            return jnp.concatenate(ws, axis=1), jnp.concatenate(dss, axis=1)

        def back(j, ws, dss):
            tout[j, p, 1] = mul(ws, gm[p]).astype(jnp.bfloat16)
            tout[j, p, 0] = mul(dss, qm[p]).astype(jnp.bfloat16)
            k_turned = kv[j, p, 0].T
            for h in range(2):
                dq_parts[h] = dq_parts[h] + mul(k_turned[halves[h]], dss[:, both[h]])

        ready = middle(0, front(0))
        for j in range(FRAMES):
            coming = front(j + 1) if j + 1 < FRAMES else None
            back(j, *ready)
            if j + 1 < FRAMES:
                ready = middle(j + 1, coming)

        for i in range(4):
            start(t_copy, t_routes, i, p)
        dq_out[p] = (jnp.concatenate(dq_parts, axis=0) * SCALE).T.astype(jnp.bfloat16)
        for i in (0, 1):
            store(i, p).start()

        @pl.when(p >= LAG)
        def _():
            near_terms(p - LAG)

    def flush(p, carry):
        near_terms(p)
        return carry

    lax.fori_loop(PAIRS - LAG, PAIRS, flush, 0)

    @each_pair
    def _(p):
        for i in range(2, 6):
            wait_recv(t_copy, t_routes, i, p)
        total = tout[OWN, p].astype(jnp.float32)
        for i in range(2, 6):
            total = total + tin[i, p].astype(jnp.float32)
        tout[OWN, p] = total.astype(jnp.bfloat16)
        for i in (2, 3):
            store(i, p).start()

    @each_pair
    def _(p):
        for i in range(6):
            wait_send(kv_copy, kv_routes, i, p)
            wait_send(t_copy, t_routes, i, p)
        for i in range(4):
            store(i, p).wait()


def hand_over(*refs):
    sources, targets, (held, sem) = refs[:4], refs[4:8], refs[8:]
    come = [pltpu.make_async_copy(sources[i], held.at[i], sem.at[0, i]) for i in range(4)]
    go = [pltpu.make_async_copy(held.at[i], targets[i], sem.at[1, i]) for i in range(4)]
    for copy in come:
        copy.start()
    for i in range(4):
        come[i].wait()
        go[i].start()
    for copy in go:
        copy.wait()


def shards(queries, keys, values, cotangent, partners, counts):
    block = jax.ShapeDtypeStruct((TOK, WIDTH), jnp.bfloat16)
    whole = pl.BlockSpec(memory_space=pl.ANY)
    low = jnp.bfloat16
    results = pl.pallas_call(
        kernel,
        out_shape=(block,) * 4,
        in_specs=[whole] * 6,
        out_specs=(whole,) * 4,
        scratch_shapes=[
            pltpu.VMEM((FRAMES, PAIRS, 2, TOK, PAIR), low),
            pltpu.VMEM((FRAMES, PAIRS, 2, TOK, PAIR), low),
            pltpu.VMEM((6, PAIRS, 2, TOK, PAIR), low),
            pltpu.VMEM((PAIRS, FRAMES, TOK, 2 * TOK), low),
            pltpu.VMEM((PAIRS, TOK, PAIR), low),
            pltpu.VMEM((PAIRS, TOK, PAIR), low),
            pltpu.VMEM((PAIRS, 2 * TOK, PAIR), low),
            pltpu.VMEM((PAIRS, 2, PAIR, TOK), low),
            pltpu.VMEM((PAIRS, 2 * TOK, PAIR), low),
            pltpu.VMEM((PAIRS, 2, PAIR, TOK), low),
            pltpu.VMEM((PAIRS, PAIR, TOK), jnp.float32),
            pltpu.VMEM((PAIRS, TOK, PAIR), low),
            pltpu.VMEM((PAIRS, TOK, PAIR), low),
            pltpu.VMEM((PAIRS, FRAMES + 1, 1, 2 * TOK), jnp.float32),
            pltpu.VMEM((PAIRS, 1, 2 * TOK), jnp.float32),
            pltpu.SMEM((FRAMES,), jnp.float32),
            pltpu.SMEM((1, SLOTS), jnp.int32),
            pltpu.SMEM((1,), jnp.int32),
            pltpu.SemaphoreType.DMA((2,)),
            pltpu.SemaphoreType.DMA((4, PAIRS)),
            pltpu.SemaphoreType.DMA((4, PAIRS)),
            pltpu.SemaphoreType.DMA((6, PAIRS)),
            pltpu.SemaphoreType.DMA((6, PAIRS)),
            pltpu.SemaphoreType.DMA((6, PAIRS)),
            pltpu.SemaphoreType.DMA((6, PAIRS)),
        ],
        compiler_params=pltpu.CompilerParams(
            collective_id=0, has_side_effects=True, vmem_limit_bytes=60 * 2**20
        ),
    )(partners, counts, queries, keys, values, cotangent)
    return pl.pallas_call(
        hand_over,
        out_shape=(block,) * 4,
        in_specs=[whole] * 4,
        out_specs=(whole,) * 4,
        scratch_shapes=[pltpu.VMEM((4, TOK, WIDTH), low), pltpu.SemaphoreType.DMA((2, 4))],
    )(*results)


def solution(mesh):
    rows = P(("clip", "frame"), None)
    return jax.shard_map(
        shards,
        mesh=mesh,
        in_specs=(rows, rows, rows, rows, rows, P(("clip", "frame"))),
        out_specs=(rows, rows, rows, rows),
        check_vma=False,
    )
```

```python
import functools
import math

import jax
import jax.numpy as jnp
from jax import lax
from jax.experimental import pallas as pl
from jax.experimental.pallas import tpu as pltpu
from jax.sharding import PartitionSpec as P

HEADS = 16
HEAD_DIM = 64
TOK = 256
WIDTH = 1024
SLOTS = 6
PAIR = 2 * HEAD_DIM
PAIRS = WIDTH // PAIR
SCALE = 1.0 / math.sqrt(HEAD_DIM)
FAR = 3e38
LAG = 3
MESH = pl.DeviceIdType.MESH

OWN = 6
FRAMES = 7
EARLY = (6, 2, 3, 4, 5)


def kernel(
    partners_hbm, counts_hbm, q_hbm, k_hbm, v_hbm, g_hbm,
    att, dq, dk, dv,
    kv, tout, tin, pb, q_in, g_in, qm, qt, gm, gt, o_t,
    mst, lst, bias, partners, counts, list_sem,
    in_sem, kv_send, kv_recv, t_send, t_recv,
):
    c = lax.axis_index("clip")
    f = lax.axis_index("frame")
    clips = lax.axis_size("clip")
    frames = lax.axis_size("frame")
    right, left = (c, f + 1), (c, f - 1)
    up = (lax.rem(c + 1, clips), f)
    down = (lax.rem(c + clips - 1, clips), f)
    has_r, has_l = f < frames - 1, f > 0
    has_rr, has_ll = f < frames - 2, f > 1
    has_both = has_r & has_l

    def columns(p):
        return pl.ds(pl.multiple_of(p * PAIR, PAIR), PAIR)

    def fetch(i, p):
        src = (k_hbm, v_hbm, q_hbm, g_hbm)[i]
        dst = kv.at[OWN, p, i] if i < 2 else (q_in, g_in)[i - 2].at[p]
        return pltpu.make_async_copy(src.at[:, columns(p)], dst, in_sem.at[i, p])

    def remote(src, dst, send, recv, device):
        return pltpu.make_async_remote_copy(
            src_ref=src, dst_ref=dst, send_sem=send, recv_sem=recv, device_id=device, device_id_type=MESH
        )

    kv_routes = [
        (OWN, 5, right, has_r, has_l),
        (OWN, 4, left, has_l, has_r),
        (OWN, 3, up, None, None),
        (OWN, 2, down, None, None),
        (5, 1, right, has_both, has_ll),
        (4, 0, left, has_both, has_rr),
    ]

    def kv_copy(i, p):
        here, there, device, _, _ = kv_routes[i]
        return remote(kv.at[here, p], kv.at[there, p], kv_send.at[i, p], kv_recv.at[there, p], device)

    t_routes = [
        (0, 0, right, has_rr, has_both),
        (1, 1, left, has_ll, has_both),
        (2, 3, up, None, None),
        (3, 2, down, None, None),
        (4, 5, right, has_r, has_l),
        (5, 4, left, has_l, has_r),
    ]

    def t_copy(i, p):
        slot, there, device, _, _ = t_routes[i]
        return remote(tout.at[slot, p], tin.at[there, p], t_send.at[i, p], t_recv.at[there, p], device)

    def when(condition, action):
        if condition is None:
            action()
        else:
            pl.when(condition)(action)

    def start(copy, routes, i, p):
        when(routes[i][3], lambda: copy(i, p).start())

    def wait_send(copy, routes, i, p):
        when(routes[i][3], lambda: copy(i, p).wait_send())

    def wait_recv(copy, routes, i, p):
        when(routes[i][4], lambda: copy(i, p).wait_recv())

    def each_pair(body):
        def step(p, carry):
            body(p)
            return carry

        lax.fori_loop(0, PAIRS, step, 0)

    lists = [
        pltpu.make_async_copy(partners_hbm, partners, list_sem.at[0]),
        pltpu.make_async_copy(counts_hbm, counts, list_sem.at[1]),
    ]
    for copy in lists:
        copy.start()

    @each_pair
    def _(p):
        for i in range(4):
            fetch(i, p).start()

    barrier = pltpu.get_barrier_semaphore()
    for device, present in ((right, has_r), (left, has_l), (up, None), (down, None)):
        when(
            present,
            functools.partial(pl.semaphore_signal, barrier, inc=1, device_id=device, device_id_type=MESH),
        )
    pl.semaphore_wait(barrier, 2 + has_r.astype(jnp.int32) + has_l.astype(jnp.int32))

    @each_pair
    def _(p):
        for i in (0, 1):
            fetch(i, p).wait()
        for i in range(4):
            start(kv_copy, kv_routes, i, p)

    for copy in lists:
        copy.wait()
    live = counts[0, 0]
    me = c * frames + f
    targets = [
        (me + 2, has_rr),
        (me - 2, has_ll),
        (up[0] * frames + f, None),
        (down[0] * frames + f, None),
        (me + 1, has_r),
        (me - 1, has_l),
    ]
    for slot, (target, present) in enumerate(targets):
        found = jnp.int32(0)
        for s in range(SLOTS):
            found = found + jnp.where((partners[0, s] == target) & (s < live), 1, 0)
        if present is not None:
            found = jnp.where(present, found, 0)
        bias[slot] = jnp.where(found > 0, 0.0, FAR).astype(jnp.float32)
    bias[OWN] = jnp.float32(0.0)

    for slot, present in ((0, has_rr), (1, has_ll), (4, has_r), (5, has_l)):

        @pl.when(jnp.logical_not(present))
        def _():
            @each_pair
            def _(p):
                kv[slot, p] = jnp.zeros(kv.shape[2:], kv.dtype)

    for slot, present in ((0, has_both), (1, has_both), (4, has_r), (5, has_l)):

        @pl.when(jnp.logical_not(present))
        def _():
            @each_pair
            def _(p):
                tin[slot, p] = jnp.zeros(tin.shape[2:], tin.dtype)

    @each_pair
    def _(p):
        for i in (2, 3):
            fetch(i, p).wait()
        lane = lax.broadcasted_iota(jnp.int32, (TOK, PAIR), 1)
        row = lax.broadcasted_iota(jnp.int32, (PAIR, TOK), 0)
        q = q_in[p].astype(jnp.float32) * SCALE
        g = g_in[p].astype(jnp.float32)
        q_turned, g_turned = q.T, g.T
        for h in range(2):
            mine = (lane < HEAD_DIM) if h == 0 else (lane >= HEAD_DIM)
            mine_t = (row < HEAD_DIM) if h == 0 else (row >= HEAD_DIM)
            rows = pl.ds(h * TOK, TOK)
            qm[p, rows, :] = jnp.where(mine, q, 0.0).astype(jnp.bfloat16)
            gm[p, rows, :] = jnp.where(mine, g, 0.0).astype(jnp.bfloat16)
            qt[p, h] = jnp.where(mine_t, q_turned, 0.0).astype(jnp.bfloat16)
            gt[p, h] = jnp.where(mine_t, g_turned, 0.0).astype(jnp.bfloat16)

    halves = [slice(h * HEAD_DIM, (h + 1) * HEAD_DIM) for h in range(2)]
    both = [slice(h * TOK, (h + 1) * TOK) for h in range(2)]

    def mul(a, b):
        return jnp.dot(a, b, preferred_element_type=jnp.float32)

    def weigh(p, slots):
        def front(j):
            return [mul(kv[j, p, 0], qt[p, h]) for h in range(2)]

        def middle(j, scores):
            tops, sums = [], []
            for h in range(2):
                top = jnp.max(scores[h], axis=0, keepdims=True)
                e = jnp.exp(scores[h] - (top + bias[j]))
                tops.append(top - bias[j])
                sums.append(jnp.sum(e, axis=0, keepdims=True))
                pb[p, j, :, both[h]] = e.astype(jnp.bfloat16)
            return jnp.concatenate(tops, axis=1), jnp.concatenate(sums, axis=1)

        def back(j):
            v_turned = kv[j, p, 1].T
            return [mul(v_turned[halves[h]], pb[p, j, :, both[h]]) for h in range(2)]

        coming = front(slots[0])
        tops, sums, parts = [], [], []
        for n, j in enumerate(slots):
            scores = coming
            if n + 1 < len(slots):
                coming = front(slots[n + 1])
            if n > 0:
                parts.append(back(slots[n - 1]))
            top, total = middle(j, scores)
            tops.append(top)
            sums.append(total)
        parts.append(back(slots[-1]))
        return tops, sums, parts

    @each_pair
    def _(p):
        for i in (0, 1):
            wait_recv(kv_copy, kv_routes, i, p)
            start(kv_copy, kv_routes, 4 + i, p)
        for i in (2, 3):
            wait_recv(kv_copy, kv_routes, i, p)
        tops, sums, parts = weigh(p, EARLY)
        top = functools.reduce(jnp.maximum, tops)
        total = jnp.zeros_like(top)
        mixed = [jnp.zeros((HEAD_DIM, TOK), jnp.float32) for _ in range(2)]
        for n, j in enumerate(EARLY):
            e = jnp.exp(tops[n] - top)
            mst[p, j] = tops[n]
            total = total + e * sums[n]
            mixed = [mixed[h] + parts[n][h] * e[:, both[h]] for h in range(2)]
        mst[p, FRAMES] = top
        lst[p] = total
        for h in range(2):
            o_t[p, halves[h]] = mixed[h]

    def near_terms(p):
        for i in (0, 1):
            wait_recv(t_copy, t_routes, i, p)
            total = tout[4 + i, p].astype(jnp.float32) + tin[i, p].astype(jnp.float32)
            tout[4 + i, p] = total.astype(jnp.bfloat16)
            start(t_copy, t_routes, 4 + i, p)

    @each_pair
    def _(p):
        for i in (4, 5):
            wait_recv(kv_copy, kv_routes, i, p)
        tops, sums, parts = weigh(p, (0, 1))
        tops = tops + [mst[p, j] for j in range(2, FRAMES)]
        early = mst[p, FRAMES]
        top = functools.reduce(jnp.maximum, [tops[0], tops[1], early])
        factors = [jnp.exp(t - top) for t in tops]
        early = jnp.exp(early - top)
        inverse = 1.0 / (early * lst[p] + factors[0] * sums[0] + factors[1] * sums[1])
        factors = [e * inverse for e in factors]
        early = early * inverse

        g_turned = gt[p, 0] + gt[p, 1]
        spread, attended = [], []
        for h in range(2):
            total = o_t[p, halves[h]] * early[:, both[h]]
            for j in (0, 1):
                total = total + parts[j][h] * factors[j][:, both[h]]
            total = total.astype(jnp.bfloat16).astype(jnp.float32)
            attended.append(total)
            spread.append(jnp.sum(g_turned[halves[h]].astype(jnp.float32) * total, axis=0, keepdims=True))
        att[:, columns(p)] = jnp.concatenate(attended, axis=0).T.astype(jnp.bfloat16)

        dq_parts = [jnp.zeros((HEAD_DIM, TOK), jnp.float32) for _ in range(2)]

        def front(j):
            return [mul(kv[j, p, 1], gt[p, h]) for h in range(2)]

        def middle(j, dws):
            ws, dss = [], []
            for h in range(2):
                w = pb[p, j, :, both[h]].astype(jnp.float32) * factors[j][:, both[h]]
                ws.append(w.astype(jnp.bfloat16))
                dss.append((w * (dws[h] - spread[h])).astype(jnp.bfloat16))
            return jnp.concatenate(ws, axis=1), jnp.concatenate(dss, axis=1)

        def back(j, ws, dss):
            tout[j, p, 1] = mul(ws, gm[p]).astype(jnp.bfloat16)
            tout[j, p, 0] = mul(dss, qm[p]).astype(jnp.bfloat16)
            k_turned = kv[j, p, 0].T
            for h in range(2):
                dq_parts[h] = dq_parts[h] + mul(k_turned[halves[h]], dss[:, both[h]])

        ready = middle(0, front(0))
        for j in range(FRAMES):
            coming = front(j + 1) if j + 1 < FRAMES else None
            back(j, *ready)
            if j + 1 < FRAMES:
                ready = middle(j + 1, coming)

        for i in range(4):
            start(t_copy, t_routes, i, p)
        dq[:, columns(p)] = (jnp.concatenate(dq_parts, axis=0) * SCALE).T.astype(jnp.bfloat16)

        @pl.when(p >= LAG)
        def _():
            near_terms(p - LAG)

    def flush(p, carry):
        near_terms(p)
        return carry

    lax.fori_loop(PAIRS - LAG, PAIRS, flush, 0)

    @each_pair
    def _(p):
        for i in range(2, 6):
            wait_recv(t_copy, t_routes, i, p)
        total = tout[OWN, p].astype(jnp.float32)
        for i in range(2, 6):
            total = total + tin[i, p].astype(jnp.float32)
        dk[:, columns(p)] = total[0].astype(jnp.bfloat16)
        dv[:, columns(p)] = total[1].astype(jnp.bfloat16)

    @each_pair
    def _(p):
        for i in range(6):
            wait_send(kv_copy, kv_routes, i, p)
            wait_send(t_copy, t_routes, i, p)


def hand_over(*refs):
    sem = refs[-1]
    half = (len(refs) - 1) // 2
    copies = [pltpu.make_async_copy(refs[i], refs[half + i], sem.at[i]) for i in range(half)]
    for copy in copies:
        copy.start()
    for copy in copies:
        copy.wait()


def shards(queries, keys, values, cotangent, partners, counts):
    block = jax.ShapeDtypeStruct((TOK, WIDTH), jnp.bfloat16)
    whole = pl.BlockSpec(memory_space=pl.ANY)
    near = pl.BlockSpec(memory_space=pltpu.VMEM)
    low = jnp.bfloat16
    results = pl.pallas_call(
        kernel,
        out_shape=(pltpu.VMEM((TOK, WIDTH), low),) * 4,
        in_specs=[whole] * 6,
        out_specs=(near,) * 4,
        scratch_shapes=[
            pltpu.VMEM((FRAMES, PAIRS, 2, TOK, PAIR), low),
            pltpu.VMEM((FRAMES, PAIRS, 2, TOK, PAIR), low),
            pltpu.VMEM((6, PAIRS, 2, TOK, PAIR), low),
            pltpu.VMEM((PAIRS, FRAMES, TOK, 2 * TOK), low),
            pltpu.VMEM((PAIRS, TOK, PAIR), low),
            pltpu.VMEM((PAIRS, TOK, PAIR), low),
            pltpu.VMEM((PAIRS, 2 * TOK, PAIR), low),
            pltpu.VMEM((PAIRS, 2, PAIR, TOK), low),
            pltpu.VMEM((PAIRS, 2 * TOK, PAIR), low),
            pltpu.VMEM((PAIRS, 2, PAIR, TOK), low),
            pltpu.VMEM((PAIRS, PAIR, TOK), jnp.float32),
            pltpu.VMEM((PAIRS, FRAMES + 1, 1, 2 * TOK), jnp.float32),
            pltpu.VMEM((PAIRS, 1, 2 * TOK), jnp.float32),
            pltpu.SMEM((FRAMES,), jnp.float32),
            pltpu.SMEM((1, SLOTS), jnp.int32),
            pltpu.SMEM((1, 1), jnp.int32),
            pltpu.SemaphoreType.DMA((2,)),
            pltpu.SemaphoreType.DMA((4, PAIRS)),
            pltpu.SemaphoreType.DMA((6, PAIRS)),
            pltpu.SemaphoreType.DMA((6, PAIRS)),
            pltpu.SemaphoreType.DMA((6, PAIRS)),
            pltpu.SemaphoreType.DMA((6, PAIRS)),
        ],
        compiler_params=pltpu.CompilerParams(
            collective_id=0, has_side_effects=True, vmem_limit_bytes=48 * 2**20
        ),
    )(
        pltpu.with_memory_space_constraint(partners, pltpu.HBM),
        counts.reshape(1, 1),
        *[pltpu.with_memory_space_constraint(x, pltpu.HBM) for x in (queries, keys, values, cotangent)],
    )
    return pl.pallas_call(
        hand_over,
        out_shape=(block,) * 4,
        in_specs=[near] * 4,
        out_specs=(whole,) * 4,
        scratch_shapes=[pltpu.SemaphoreType.DMA((4,))],
    )(*[pltpu.with_memory_space_constraint(x, pltpu.VMEM) for x in results])


def solution(mesh):
    rows = P(("clip", "frame"), None)
    return jax.shard_map(
        shards,
        mesh=mesh,
        in_specs=(rows, rows, rows, rows, rows, P(("clip", "frame"))),
        out_specs=(rows, rows, rows, rows),
        check_vma=False,
    )
```

```python
import functools
import math

import jax
import jax.numpy as jnp
from jax import lax
from jax.experimental import pallas as pl
from jax.experimental.pallas import tpu as pltpu
from jax.sharding import PartitionSpec as P

HEADS = 16
HEAD_DIM = 64
TOK = 256
WIDTH = 1024
SLOTS = 6
PAIR = 2 * HEAD_DIM
PAIRS = WIDTH // PAIR
SCALE = 1.0 / math.sqrt(HEAD_DIM)
FAR = 3e38
LAG = 3
MESH = pl.DeviceIdType.MESH

SEAMS = ((7, 8), (15, 16), (23, 24))
RELAYS = ((31, 23, 31), (0, 8, 0))
DETOURS = ((2, 2, 4), (4, 2, 2))
MOST = 4
RELAY_AT = (2, 2, 3)
HEADSTART = 2

OWN = 6
FRAMES = 7
EARLY = (6, 2, 3, 4, 5)


def kernel(
    partners_hbm, counts_hbm, q_hbm, k_hbm, v_hbm, g_hbm,
    att, dq, dk, dv,
    kv, tout, tin, pb, q_in, g_in, qm, qt, gm, gt, o_t,
    mst, lst, bias, partners, counts, list_sem,
    in_sem, kv_send, kv_recv, t_send, t_recv,
    relayed, relay_send, relay_recv, seam_ok, relay_ok, far_ok,
):
    c = lax.axis_index("clip")
    f = lax.axis_index("frame")
    clips = lax.axis_size("clip")
    frames = lax.axis_size("frame")
    right, left = (c, f + 1), (c, f - 1)
    up = (lax.rem(c + 1, clips), f)
    down = (lax.rem(c + clips - 1, clips), f)
    has_r, has_l = f < frames - 1, f > 0
    has_rr, has_ll = f < frames - 2, f > 1
    has_both = has_r & has_l

    def is_any(*ids):
        return functools.reduce(jnp.logical_or, [f == i for i in ids])

    before, after = (is_any(*(seam[side] for seam in SEAMS)) for side in range(2))

    def columns(p):
        return pl.ds(pl.multiple_of(p * PAIR, PAIR), PAIR)

    def fetch(i, p):
        src = (k_hbm, v_hbm, q_hbm, g_hbm)[i]
        dst = kv.at[OWN, p, i] if i < 2 else (q_in, g_in)[i - 2].at[p]
        return pltpu.make_async_copy(src.at[:, columns(p)], dst, in_sem.at[i, p])

    def remote(src, dst, send, recv, device):
        return pltpu.make_async_remote_copy(
            src_ref=src, dst_ref=dst, send_sem=send, recv_sem=recv, device_id=device, device_id_type=MESH
        )

    kv_routes = [
        (OWN, 5, right, has_r, has_l),
        (OWN, 4, left, has_l, has_r),
        (OWN, 3, up, None, None),
        (OWN, 2, down, None, None),
        (5, 1, right, has_both, has_ll),
        (4, 0, left, has_both, has_rr),
    ]

    def kv_copy(i, p):
        here, there, device, _, _ = kv_routes[i]
        return remote(kv.at[here, p], kv.at[there, p], kv_send.at[i, p], kv_recv.at[there, p], device)

    t_routes = [
        (0, 0, right, has_rr, has_both),
        (1, 1, left, has_ll, has_both),
        (2, 3, up, None, None),
        (3, 2, down, None, None),
        (4, 5, right, has_r, has_l),
        (5, 4, left, has_l, has_r),
    ]

    def t_copy(i, p):
        slot, there, device, _, _ = t_routes[i]
        return remote(tout.at[slot, p], tin.at[there, p], t_send.at[i, p], t_recv.at[there, p], device)

    def when(condition, action):
        if condition is None:
            action()
        else:
            pl.when(condition)(action)

    def start(copy, routes, i, p):
        when(routes[i][3], lambda: copy(i, p).start())

    def wait_send(copy, routes, i, p):
        when(routes[i][3], lambda: copy(i, p).wait_send())

    def wait_recv(copy, routes, i, p):
        when(routes[i][4], lambda: copy(i, p).wait_recv())

    def each_pair(body):
        def step(p, carry):
            body(p)
            return carry

        lax.fori_loop(0, PAIRS, step, 0)

    lists = [
        pltpu.make_async_copy(partners_hbm, partners, list_sem.at[0]),
        pltpu.make_async_copy(counts_hbm, counts, list_sem.at[1]),
    ]
    for copy in lists:
        copy.start()

    @each_pair
    def _(p):
        for i in range(4):
            fetch(i, p).start()

    def signal(semaphore, device):
        pl.semaphore_signal(semaphore, inc=1, device_id=device, device_id_type=MESH)

    def signal_frames(condition, *ids):
        @pl.when(condition)
        def _():
            for i in ids:
                signal(barrier, (c, i))

    barrier = pltpu.get_barrier_semaphore()
    pl.when(has_r & jnp.logical_not(before))(lambda: signal(barrier, right))
    pl.when(has_l)(lambda: signal(barrier, left))
    signal(barrier, up)
    signal(barrier, down)
    signal_frames(is_any(7, 8, 23, 24), 0, 31)
    signal_frames(f == 15, 23)
    signal_frames(f == 16, 23, 8)
    signal_frames(f == 8, 15)

    def amount(condition, count):
        return count * condition.astype(jnp.int32)

    greeted = 2 + amount(has_r, 1) + amount(has_l & jnp.logical_not(after), 1)
    greeted = greeted + amount(is_any(0, 31), 4) + amount(f == 23, 2) + amount(is_any(8, 15), 1)
    pl.semaphore_wait(barrier, greeted)
    pl.when(before)(lambda: signal(seam_ok, right))
    pl.when(f == 15)(lambda: signal(far_ok, (c, 8)))
    sides = [(side, k) for k in range(len(SEAMS)) for side in range(2)]
    for side, k in sides:
        pl.when(f == RELAYS[side][k])(lambda: signal(relay_ok, (c, SEAMS[k][side])))

    def detour(side, k, n):
        pair = PAIRS - DETOURS[side][k] + n
        device = (c, RELAYS[side][k])
        return remote(kv.at[OWN, pair], relayed.at[k, n], kv_send.at[side, pair], relay_recv.at[k, n], device)

    def relay(side, k, n):
        pair, slot = PAIRS - DETOURS[side][k] + n, 5 - side
        device = (c, SEAMS[k][1 - side])
        return remote(relayed.at[k, n], kv.at[slot, pair], relay_send.at[k, n], kv_recv.at[slot, pair], device)

    @each_pair
    def _(p):
        for i in (0, 1):
            fetch(i, p).wait()

    direct = [
        PAIRS - sum(amount(f == seam[side], count) for seam, count in zip(SEAMS, DETOURS[side])) for side in range(2)
    ]

    def send_own(p, carry):
        pl.when(has_r & (p < direct[0]))(lambda: kv_copy(0, p).start())
        pl.when(has_l & (p < direct[1]) & jnp.logical_not(after & (p < HEADSTART)))(lambda: kv_copy(1, p).start())
        for i in (2, 3):
            kv_copy(i, p).start()
        return carry

    lax.fori_loop(0, HEADSTART, send_own, 0)

    @pl.when(after)
    def _():
        pl.semaphore_wait(seam_ok, 1)
        for p in range(HEADSTART):
            kv_copy(1, p).start()

    for side, k in sides:

        @pl.when(f == SEAMS[k][side])
        def _():
            pl.semaphore_wait(relay_ok, 1)
            for n in range(DETOURS[side][k]):
                detour(side, k, n).start()

    lax.fori_loop(HEADSTART, PAIRS, send_own, 0)

    def pass_on(k):
        for side in range(2):

            @pl.when(f == RELAYS[side][k])
            def _():
                if RELAYS[side][k] == 8:
                    pl.semaphore_wait(far_ok, 1)
                for n in range(DETOURS[side][k]):
                    detour(side, k, n).wait_recv()
                    relay(side, k, n).start()

    for copy in lists:
        copy.wait()
    live = counts[0, 0]
    me = c * frames + f
    targets = [
        (me + 2, has_rr),
        (me - 2, has_ll),
        (up[0] * frames + f, None),
        (down[0] * frames + f, None),
        (me + 1, has_r),
        (me - 1, has_l),
    ]
    for slot, (target, present) in enumerate(targets):
        found = jnp.int32(0)
        for s in range(SLOTS):
            found = found + jnp.where((partners[0, s] == target) & (s < live), 1, 0)
        if present is not None:
            found = jnp.where(present, found, 0)
        bias[slot] = jnp.where(found > 0, 0.0, FAR).astype(jnp.float32)
    bias[OWN] = jnp.float32(0.0)

    for slot, present in ((0, has_rr), (1, has_ll), (4, has_r), (5, has_l)):

        @pl.when(jnp.logical_not(present))
        def _():
            @each_pair
            def _(p):
                kv[slot, p] = jnp.zeros(kv.shape[2:], kv.dtype)

    for slot, present in ((0, has_both), (1, has_both), (4, has_r), (5, has_l)):

        @pl.when(jnp.logical_not(present))
        def _():
            @each_pair
            def _(p):
                tin[slot, p] = jnp.zeros(tin.shape[2:], tin.dtype)

    @each_pair
    def _(p):
        for i in (2, 3):
            fetch(i, p).wait()
        lane = lax.broadcasted_iota(jnp.int32, (TOK, PAIR), 1)
        row = lax.broadcasted_iota(jnp.int32, (PAIR, TOK), 0)
        q = q_in[p].astype(jnp.float32) * SCALE
        g = g_in[p].astype(jnp.float32)
        q_turned, g_turned = q.T, g.T
        for h in range(2):
            mine = (lane < HEAD_DIM) if h == 0 else (lane >= HEAD_DIM)
            mine_t = (row < HEAD_DIM) if h == 0 else (row >= HEAD_DIM)
            rows = pl.ds(h * TOK, TOK)
            qm[p, rows, :] = jnp.where(mine, q, 0.0).astype(jnp.bfloat16)
            gm[p, rows, :] = jnp.where(mine, g, 0.0).astype(jnp.bfloat16)
            qt[p, h] = jnp.where(mine_t, q_turned, 0.0).astype(jnp.bfloat16)
            gt[p, h] = jnp.where(mine_t, g_turned, 0.0).astype(jnp.bfloat16)

    halves = [slice(h * HEAD_DIM, (h + 1) * HEAD_DIM) for h in range(2)]
    both = [slice(h * TOK, (h + 1) * TOK) for h in range(2)]

    def mul(a, b):
        return jnp.dot(a, b, preferred_element_type=jnp.float32)

    def weigh(p, slots):
        def front(j):
            return [mul(kv[j, p, 0], qt[p, h]) for h in range(2)]

        def middle(j, scores):
            tops, sums = [], []
            for h in range(2):
                top = jnp.max(scores[h], axis=0, keepdims=True)
                e = jnp.exp(scores[h] - (top + bias[j]))
                tops.append(top - bias[j])
                sums.append(jnp.sum(e, axis=0, keepdims=True))
                pb[p, j, :, both[h]] = e.astype(jnp.bfloat16)
            return jnp.concatenate(tops, axis=1), jnp.concatenate(sums, axis=1)

        def back(j):
            v_turned = kv[j, p, 1].T
            return [mul(v_turned[halves[h]], pb[p, j, :, both[h]]) for h in range(2)]

        coming = front(slots[0])
        tops, sums, parts = [], [], []
        for n, j in enumerate(slots):
            scores = coming
            if n + 1 < len(slots):
                coming = front(slots[n + 1])
            if n > 0:
                parts.append(back(slots[n - 1]))
            top, total = middle(j, scores)
            tops.append(top)
            sums.append(total)
        parts.append(back(slots[-1]))
        return tops, sums, parts

    @each_pair
    def _(p):
        for i in (0, 1):
            wait_recv(kv_copy, kv_routes, i, p)
            start(kv_copy, kv_routes, 4 + i, p)
        for k in range(len(SEAMS)):
            pl.when(p == RELAY_AT[k])(lambda: pass_on(k))
        for i in (2, 3):
            wait_recv(kv_copy, kv_routes, i, p)
        tops, sums, parts = weigh(p, EARLY)
        top = functools.reduce(jnp.maximum, tops)
        total = jnp.zeros_like(top)
        mixed = [jnp.zeros((HEAD_DIM, TOK), jnp.float32) for _ in range(2)]
        for n, j in enumerate(EARLY):
            e = jnp.exp(tops[n] - top)
            mst[p, j] = tops[n]
            total = total + e * sums[n]
            mixed = [mixed[h] + parts[n][h] * e[:, both[h]] for h in range(2)]
        mst[p, FRAMES] = top
        lst[p] = total
        for h in range(2):
            o_t[p, halves[h]] = mixed[h]

    def near_terms(p):
        for i in (0, 1):
            wait_recv(t_copy, t_routes, i, p)
            total = tout[4 + i, p].astype(jnp.float32) + tin[i, p].astype(jnp.float32)
            tout[4 + i, p] = total.astype(jnp.bfloat16)
            start(t_copy, t_routes, 4 + i, p)

    @each_pair
    def _(p):
        for i in (4, 5):
            wait_recv(kv_copy, kv_routes, i, p)
        tops, sums, parts = weigh(p, (0, 1))
        tops = tops + [mst[p, j] for j in range(2, FRAMES)]
        early = mst[p, FRAMES]
        top = functools.reduce(jnp.maximum, [tops[0], tops[1], early])
        factors = [jnp.exp(t - top) for t in tops]
        early = jnp.exp(early - top)
        inverse = 1.0 / (early * lst[p] + factors[0] * sums[0] + factors[1] * sums[1])
        factors = [e * inverse for e in factors]
        early = early * inverse

        g_turned = gt[p, 0] + gt[p, 1]
        spread, attended = [], []
        for h in range(2):
            total = o_t[p, halves[h]] * early[:, both[h]]
            for j in (0, 1):
                total = total + parts[j][h] * factors[j][:, both[h]]
            total = total.astype(jnp.bfloat16).astype(jnp.float32)
            attended.append(total)
            spread.append(jnp.sum(g_turned[halves[h]].astype(jnp.float32) * total, axis=0, keepdims=True))
        att[:, columns(p)] = jnp.concatenate(attended, axis=0).T.astype(jnp.bfloat16)

        dq_parts = [jnp.zeros((HEAD_DIM, TOK), jnp.float32) for _ in range(2)]

        def front(j):
            return [mul(kv[j, p, 1], gt[p, h]) for h in range(2)]

        def middle(j, dws):
            ws, dss = [], []
            for h in range(2):
                w = pb[p, j, :, both[h]].astype(jnp.float32) * factors[j][:, both[h]]
                ws.append(w.astype(jnp.bfloat16))
                dss.append((w * (dws[h] - spread[h])).astype(jnp.bfloat16))
            return jnp.concatenate(ws, axis=1), jnp.concatenate(dss, axis=1)

        def back(j, ws, dss):
            tout[j, p, 1] = mul(ws, gm[p]).astype(jnp.bfloat16)
            tout[j, p, 0] = mul(dss, qm[p]).astype(jnp.bfloat16)
            k_turned = kv[j, p, 0].T
            for h in range(2):
                dq_parts[h] = dq_parts[h] + mul(k_turned[halves[h]], dss[:, both[h]])

        ready = middle(0, front(0))
        for j in range(FRAMES):
            coming = front(j + 1) if j + 1 < FRAMES else None
            back(j, *ready)
            if j + 1 < FRAMES:
                ready = middle(j + 1, coming)

        for i in range(4):
            start(t_copy, t_routes, i, p)
        dq[:, columns(p)] = (jnp.concatenate(dq_parts, axis=0) * SCALE).T.astype(jnp.bfloat16)

        @pl.when(p >= LAG)
        def _():
            near_terms(p - LAG)

    def flush(p, carry):
        near_terms(p)
        return carry

    lax.fori_loop(PAIRS - LAG, PAIRS, flush, 0)

    @each_pair
    def _(p):
        for i in range(2, 6):
            wait_recv(t_copy, t_routes, i, p)
        total = tout[OWN, p].astype(jnp.float32)
        for i in range(2, 6):
            total = total + tin[i, p].astype(jnp.float32)
        dk[:, columns(p)] = total[0].astype(jnp.bfloat16)
        dv[:, columns(p)] = total[1].astype(jnp.bfloat16)

    @each_pair
    def _(p):
        for i in range(6):
            wait_send(kv_copy, kv_routes, i, p)
            wait_send(t_copy, t_routes, i, p)

    for side, k in sides:

        @pl.when(f == RELAYS[side][k])
        def _():
            for n in range(DETOURS[side][k]):
                relay(side, k, n).wait_send()


def hand_over(*refs):
    sem = refs[-1]
    half = (len(refs) - 1) // 2
    copies = [pltpu.make_async_copy(refs[i], refs[half + i], sem.at[i]) for i in range(half)]
    for copy in copies:
        copy.start()
    for copy in copies:
        copy.wait()


def shards(queries, keys, values, cotangent, partners, counts):
    block = jax.ShapeDtypeStruct((TOK, WIDTH), jnp.bfloat16)
    whole = pl.BlockSpec(memory_space=pl.ANY)
    near = pl.BlockSpec(memory_space=pltpu.VMEM)
    low = jnp.bfloat16
    results = pl.pallas_call(
        kernel,
        out_shape=(pltpu.VMEM((TOK, WIDTH), low),) * 4,
        in_specs=[whole] * 6,
        out_specs=(near,) * 4,
        scratch_shapes=[
            pltpu.VMEM((FRAMES, PAIRS, 2, TOK, PAIR), low),
            pltpu.VMEM((FRAMES, PAIRS, 2, TOK, PAIR), low),
            pltpu.VMEM((6, PAIRS, 2, TOK, PAIR), low),
            pltpu.VMEM((PAIRS, FRAMES, TOK, 2 * TOK), low),
            pltpu.VMEM((PAIRS, TOK, PAIR), low),
            pltpu.VMEM((PAIRS, TOK, PAIR), low),
            pltpu.VMEM((PAIRS, 2 * TOK, PAIR), low),
            pltpu.VMEM((PAIRS, 2, PAIR, TOK), low),
            pltpu.VMEM((PAIRS, 2 * TOK, PAIR), low),
            pltpu.VMEM((PAIRS, 2, PAIR, TOK), low),
            pltpu.VMEM((PAIRS, PAIR, TOK), jnp.float32),
            pltpu.VMEM((PAIRS, FRAMES + 1, 1, 2 * TOK), jnp.float32),
            pltpu.VMEM((PAIRS, 1, 2 * TOK), jnp.float32),
            pltpu.SMEM((FRAMES,), jnp.float32),
            pltpu.SMEM((1, SLOTS), jnp.int32),
            pltpu.SMEM((1, 1), jnp.int32),
            pltpu.SemaphoreType.DMA((2,)),
            pltpu.SemaphoreType.DMA((4, PAIRS)),
            pltpu.SemaphoreType.DMA((6, PAIRS)),
            pltpu.SemaphoreType.DMA((6, PAIRS)),
            pltpu.SemaphoreType.DMA((6, PAIRS)),
            pltpu.SemaphoreType.DMA((6, PAIRS)),
            pltpu.VMEM((len(SEAMS), MOST, 2, TOK, PAIR), low),
            pltpu.SemaphoreType.DMA((len(SEAMS), MOST)),
            pltpu.SemaphoreType.DMA((len(SEAMS), MOST)),
            pltpu.SemaphoreType.REGULAR,
            pltpu.SemaphoreType.REGULAR,
            pltpu.SemaphoreType.REGULAR,
        ],
        compiler_params=pltpu.CompilerParams(
            collective_id=0, has_side_effects=True, vmem_limit_bytes=48 * 2**20
        ),
    )(
        pltpu.with_memory_space_constraint(partners, pltpu.HBM),
        counts.reshape(1, 1),
        *[pltpu.with_memory_space_constraint(x, pltpu.HBM) for x in (queries, keys, values, cotangent)],
    )
    return pl.pallas_call(
        hand_over,
        out_shape=(block,) * 4,
        in_specs=[near] * 4,
        out_specs=(whole,) * 4,
        scratch_shapes=[pltpu.SemaphoreType.DMA((4,))],
    )(*[pltpu.with_memory_space_constraint(x, pltpu.VMEM) for x in results])


def solution(mesh):
    rows = P(("clip", "frame"), None)
    return jax.shard_map(
        shards,
        mesh=mesh,
        in_specs=(rows, rows, rows, rows, rows, P(("clip", "frame"))),
        out_specs=(rows, rows, rows, rows),
        check_vma=False,
    )
```

```python
import functools
import math

import jax
import jax.numpy as jnp
from jax import lax
from jax.experimental import pallas as pl
from jax.experimental.pallas import tpu as pltpu
from jax.sharding import PartitionSpec as P

HEADS = 16
HEAD_DIM = 64
TOK = 256
WIDTH = 1024
SLOTS = 6
PAIR = 2 * HEAD_DIM
PAIRS = WIDTH // PAIR
SCALE = 1.0 / math.sqrt(HEAD_DIM)
FAR = 3e38
LAG = 3
MESH = pl.DeviceIdType.MESH

SEAMS = ((7, 8), (15, 16), (23, 24))
RELAYS = ((31, 23, 31), (0, 8, 0))
DETOURS = ((2, 2, 4), (4, 2, 2))
MOST = 4
RELAY_AT = (2, 2, 3)
HEADSTART = 2

OWN = 6
FRAMES = 7
EARLY = (6, 2, 3, 4, 5)


def kernel(
    partners_hbm, counts_hbm, q_hbm, k_hbm, v_hbm, g_hbm,
    att, dq, dk, dv,
    kv, tout, tin, pb, q_in, g_in, qm, qt, gm, gt, o_t,
    mst, lst, bias, partners, counts, list_sem,
    in_sem, kv_send, kv_recv, t_send, t_recv,
    relayed, relay_send, relay_recv, seam_ok, relay_ok, far_ok,
):
    c = lax.axis_index("clip")
    f = lax.axis_index("frame")
    clips = lax.axis_size("clip")
    frames = lax.axis_size("frame")
    right, left = (c, f + 1), (c, f - 1)
    up = (lax.rem(c + 1, clips), f)
    down = (lax.rem(c + clips - 1, clips), f)
    has_r, has_l = f < frames - 1, f > 0
    has_rr, has_ll = f < frames - 2, f > 1
    has_both = has_r & has_l

    def is_any(*ids):
        return functools.reduce(jnp.logical_or, [f == i for i in ids])

    before, after = (is_any(*(seam[side] for seam in SEAMS)) for side in range(2))

    def columns(p):
        return pl.ds(pl.multiple_of(p * PAIR, PAIR), PAIR)

    def fetch(i, p):
        src = (k_hbm, v_hbm, q_hbm, g_hbm)[i]
        dst = kv.at[OWN, p, i] if i < 2 else (q_in, g_in)[i - 2].at[p]
        return pltpu.make_async_copy(src.at[:, columns(p)], dst, in_sem.at[i, p])

    def remote(src, dst, send, recv, device):
        return pltpu.make_async_remote_copy(
            src_ref=src, dst_ref=dst, send_sem=send, recv_sem=recv, device_id=device, device_id_type=MESH
        )

    kv_routes = [
        (OWN, 5, right, has_r, has_l),
        (OWN, 4, left, has_l, has_r),
        (OWN, 3, up, None, None),
        (OWN, 2, down, None, None),
        (5, 1, right, has_both, has_ll),
        (4, 0, left, has_both, has_rr),
    ]

    def kv_copy(i, p):
        here, there, device, _, _ = kv_routes[i]
        return remote(kv.at[here, p], kv.at[there, p], kv_send.at[i, p], kv_recv.at[there, p], device)

    t_routes = [
        (0, 0, right, has_rr, has_both),
        (1, 1, left, has_ll, has_both),
        (2, 3, up, None, None),
        (3, 2, down, None, None),
        (4, 5, right, has_r, has_l),
        (5, 4, left, has_l, has_r),
    ]

    def t_copy(i, p):
        slot, there, device, _, _ = t_routes[i]
        return remote(tout.at[slot, p], tin.at[there, p], t_send.at[i, p], t_recv.at[there, p], device)

    def when(condition, action):
        if condition is None:
            action()
        else:
            pl.when(condition)(action)

    def start(copy, routes, i, p):
        when(routes[i][3], lambda: copy(i, p).start())

    def wait_send(copy, routes, i, p):
        when(routes[i][3], lambda: copy(i, p).wait_send())

    def wait_recv(copy, routes, i, p):
        when(routes[i][4], lambda: copy(i, p).wait_recv())

    def each_pair(body):
        def step(p, carry):
            body(p)
            return carry

        lax.fori_loop(0, PAIRS, step, 0)

    def signal(semaphore, device):
        pl.semaphore_signal(semaphore, inc=1, device_id=device, device_id_type=MESH)

    def signal_frames(condition, *ids):
        @pl.when(condition)
        def _():
            for i in ids:
                signal(barrier, (c, i))

    barrier = pltpu.get_barrier_semaphore()
    pl.when(has_r & jnp.logical_not(before))(lambda: signal(barrier, right))
    pl.when(has_l)(lambda: signal(barrier, left))
    signal(barrier, up)
    signal(barrier, down)
    signal_frames(is_any(7, 8, 23, 24), 0, 31)
    signal_frames(f == 15, 23)
    signal_frames(f == 16, 23, 8)
    signal_frames(f == 8, 15)

    @each_pair
    def _(p):
        for i in (0, 1):
            fetch(i, p).start()

    def amount(condition, count):
        return count * condition.astype(jnp.int32)

    greeted = 2 + amount(has_r, 1) + amount(has_l & jnp.logical_not(after), 1)
    greeted = greeted + amount(is_any(0, 31), 4) + amount(f == 23, 2) + amount(is_any(8, 15), 1)
    pl.semaphore_wait(barrier, greeted)
    pl.when(before)(lambda: signal(seam_ok, right))
    pl.when(f == 15)(lambda: signal(far_ok, (c, 8)))
    sides = [(side, k) for k in range(len(SEAMS)) for side in range(2)]
    for side, k in sides:
        pl.when(f == RELAYS[side][k])(lambda: signal(relay_ok, (c, SEAMS[k][side])))

    def detour(side, k, n):
        pair = PAIRS - DETOURS[side][k] + n
        device = (c, RELAYS[side][k])
        return remote(kv.at[OWN, pair], relayed.at[k, n], kv_send.at[side, pair], relay_recv.at[k, n], device)

    def relay(side, k, n):
        pair, slot = PAIRS - DETOURS[side][k] + n, 5 - side
        device = (c, SEAMS[k][1 - side])
        return remote(relayed.at[k, n], kv.at[slot, pair], relay_send.at[k, n], kv_recv.at[slot, pair], device)

    direct = [
        PAIRS - sum(amount(f == seam[side], count) for seam, count in zip(SEAMS, DETOURS[side])) for side in range(2)
    ]

    def send_own(p, carry):
        pl.when(has_r & (p < direct[0]))(lambda: kv_copy(0, p).start())
        pl.when(has_l & (p < direct[1]) & jnp.logical_not(after & (p < HEADSTART)))(lambda: kv_copy(1, p).start())
        for i in (2, 3):
            kv_copy(i, p).start()
        return carry

    def fetched(p, carry):
        for i in (0, 1):
            fetch(i, p).wait()
        return carry

    lax.fori_loop(0, HEADSTART, lambda p, carry: send_own(p, fetched(p, carry)), 0)
    lax.fori_loop(HEADSTART, PAIRS, fetched, 0)

    @pl.when(after)
    def _():
        pl.semaphore_wait(seam_ok, 1)
        for p in range(HEADSTART):
            kv_copy(1, p).start()

    for side, k in sides:

        @pl.when(f == SEAMS[k][side])
        def _():
            pl.semaphore_wait(relay_ok, 1)
            for n in range(DETOURS[side][k]):
                detour(side, k, n).start()

    lax.fori_loop(HEADSTART, PAIRS, send_own, 0)

    lists = [
        pltpu.make_async_copy(partners_hbm, partners, list_sem.at[0]),
        pltpu.make_async_copy(counts_hbm, counts, list_sem.at[1]),
    ]
    for copy in lists:
        copy.start()

    @each_pair
    def _(p):
        for i in (2, 3):
            fetch(i, p).start()

    def pass_on(k):
        for side in range(2):

            @pl.when(f == RELAYS[side][k])
            def _():
                if RELAYS[side][k] == 8:
                    pl.semaphore_wait(far_ok, 1)
                for n in range(DETOURS[side][k]):
                    detour(side, k, n).wait_recv()
                    relay(side, k, n).start()

    for copy in lists:
        copy.wait()
    live = counts[0, 0]
    me = c * frames + f
    targets = [
        (me + 2, has_rr),
        (me - 2, has_ll),
        (up[0] * frames + f, None),
        (down[0] * frames + f, None),
        (me + 1, has_r),
        (me - 1, has_l),
    ]
    for slot, (target, present) in enumerate(targets):
        found = jnp.int32(0)
        for s in range(SLOTS):
            found = found + jnp.where((partners[0, s] == target) & (s < live), 1, 0)
        if present is not None:
            found = jnp.where(present, found, 0)
        bias[slot] = jnp.where(found > 0, 0.0, FAR).astype(jnp.float32)
    bias[OWN] = jnp.float32(0.0)

    for slot, present in ((0, has_rr), (1, has_ll), (4, has_r), (5, has_l)):

        @pl.when(jnp.logical_not(present))
        def _():
            @each_pair
            def _(p):
                kv[slot, p] = jnp.zeros(kv.shape[2:], kv.dtype)

    for slot, present in ((0, has_both), (1, has_both), (4, has_r), (5, has_l)):

        @pl.when(jnp.logical_not(present))
        def _():
            @each_pair
            def _(p):
                tin[slot, p] = jnp.zeros(tin.shape[2:], tin.dtype)

    @each_pair
    def _(p):
        for i in (2, 3):
            fetch(i, p).wait()
        lane = lax.broadcasted_iota(jnp.int32, (TOK, PAIR), 1)
        row = lax.broadcasted_iota(jnp.int32, (PAIR, TOK), 0)
        q = q_in[p].astype(jnp.float32) * SCALE
        g = g_in[p].astype(jnp.float32)
        q_turned, g_turned = q.T, g.T
        for h in range(2):
            mine = (lane < HEAD_DIM) if h == 0 else (lane >= HEAD_DIM)
            mine_t = (row < HEAD_DIM) if h == 0 else (row >= HEAD_DIM)
            rows = pl.ds(h * TOK, TOK)
            qm[p, rows, :] = jnp.where(mine, q, 0.0).astype(jnp.bfloat16)
            gm[p, rows, :] = jnp.where(mine, g, 0.0).astype(jnp.bfloat16)
            qt[p, h] = jnp.where(mine_t, q_turned, 0.0).astype(jnp.bfloat16)
            gt[p, h] = jnp.where(mine_t, g_turned, 0.0).astype(jnp.bfloat16)

    halves = [slice(h * HEAD_DIM, (h + 1) * HEAD_DIM) for h in range(2)]
    both = [slice(h * TOK, (h + 1) * TOK) for h in range(2)]

    def mul(a, b):
        return jnp.dot(a, b, preferred_element_type=jnp.float32)

    def weigh(p, slots):
        def front(j):
            return [mul(kv[j, p, 0], qt[p, h]) for h in range(2)]

        def middle(j, scores):
            tops, sums = [], []
            for h in range(2):
                top = jnp.max(scores[h], axis=0, keepdims=True)
                e = jnp.exp(scores[h] - (top + bias[j]))
                tops.append(top - bias[j])
                sums.append(jnp.sum(e, axis=0, keepdims=True))
                pb[p, j, :, both[h]] = e.astype(jnp.bfloat16)
            return jnp.concatenate(tops, axis=1), jnp.concatenate(sums, axis=1)

        def back(j):
            v_turned = kv[j, p, 1].T
            return [mul(v_turned[halves[h]], pb[p, j, :, both[h]]) for h in range(2)]

        coming = front(slots[0])
        tops, sums, parts = [], [], []
        for n, j in enumerate(slots):
            scores = coming
            if n + 1 < len(slots):
                coming = front(slots[n + 1])
            if n > 0:
                parts.append(back(slots[n - 1]))
            top, total = middle(j, scores)
            tops.append(top)
            sums.append(total)
        parts.append(back(slots[-1]))
        return tops, sums, parts

    @each_pair
    def _(p):
        for i in (0, 1):
            wait_recv(kv_copy, kv_routes, i, p)
            start(kv_copy, kv_routes, 4 + i, p)
        for k in range(len(SEAMS)):
            pl.when(p == RELAY_AT[k])(lambda: pass_on(k))
        for i in (2, 3):
            wait_recv(kv_copy, kv_routes, i, p)
        tops, sums, parts = weigh(p, EARLY)
        top = functools.reduce(jnp.maximum, tops)
        total = jnp.zeros_like(top)
        mixed = [jnp.zeros((HEAD_DIM, TOK), jnp.float32) for _ in range(2)]
        for n, j in enumerate(EARLY):
            e = jnp.exp(tops[n] - top)
            mst[p, j] = tops[n]
            total = total + e * sums[n]
            mixed = [mixed[h] + parts[n][h] * e[:, both[h]] for h in range(2)]
        mst[p, FRAMES] = top
        lst[p] = total
        for h in range(2):
            o_t[p, halves[h]] = mixed[h]

    def near_terms(p):
        for i in (0, 1):
            wait_recv(t_copy, t_routes, i, p)
            total = tout[4 + i, p].astype(jnp.float32) + tin[i, p].astype(jnp.float32)
            tout[4 + i, p] = total.astype(jnp.bfloat16)
            start(t_copy, t_routes, 4 + i, p)

    @each_pair
    def _(p):
        for i in (4, 5):
            wait_recv(kv_copy, kv_routes, i, p)
        tops, sums, parts = weigh(p, (0, 1))
        tops = tops + [mst[p, j] for j in range(2, FRAMES)]
        early = mst[p, FRAMES]
        top = functools.reduce(jnp.maximum, [tops[0], tops[1], early])
        factors = [jnp.exp(t - top) for t in tops]
        early = jnp.exp(early - top)
        inverse = 1.0 / (early * lst[p] + factors[0] * sums[0] + factors[1] * sums[1])
        factors = [e * inverse for e in factors]
        early = early * inverse

        g_turned = gt[p, 0] + gt[p, 1]
        spread, attended = [], []
        for h in range(2):
            total = o_t[p, halves[h]] * early[:, both[h]]
            for j in (0, 1):
                total = total + parts[j][h] * factors[j][:, both[h]]
            total = total.astype(jnp.bfloat16).astype(jnp.float32)
            attended.append(total)
            spread.append(jnp.sum(g_turned[halves[h]].astype(jnp.float32) * total, axis=0, keepdims=True))
        att[:, columns(p)] = jnp.concatenate(attended, axis=0).T.astype(jnp.bfloat16)

        dq_parts = [jnp.zeros((HEAD_DIM, TOK), jnp.float32) for _ in range(2)]

        def front(j):
            return [mul(kv[j, p, 1], gt[p, h]) for h in range(2)]

        def middle(j, dws):
            ws, dss = [], []
            for h in range(2):
                w = pb[p, j, :, both[h]].astype(jnp.float32) * factors[j][:, both[h]]
                ws.append(w.astype(jnp.bfloat16))
                dss.append((w * (dws[h] - spread[h])).astype(jnp.bfloat16))
            return jnp.concatenate(ws, axis=1), jnp.concatenate(dss, axis=1)

        def back(j, ws, dss):
            tout[j, p, 1] = mul(ws, gm[p]).astype(jnp.bfloat16)
            tout[j, p, 0] = mul(dss, qm[p]).astype(jnp.bfloat16)
            k_turned = kv[j, p, 0].T
            for h in range(2):
                dq_parts[h] = dq_parts[h] + mul(k_turned[halves[h]], dss[:, both[h]])

        ready = middle(0, front(0))
        for j in range(FRAMES):
            coming = front(j + 1) if j + 1 < FRAMES else None
            back(j, *ready)
            if j + 1 < FRAMES:
                ready = middle(j + 1, coming)

        for i in range(4):
            start(t_copy, t_routes, i, p)
        dq[:, columns(p)] = (jnp.concatenate(dq_parts, axis=0) * SCALE).T.astype(jnp.bfloat16)

        @pl.when(p >= LAG)
        def _():
            near_terms(p - LAG)

    def flush(p, carry):
        near_terms(p)
        return carry

    lax.fori_loop(PAIRS - LAG, PAIRS, flush, 0)

    for side, k in sides:

        @pl.when(f == RELAYS[side][k])
        def _():
            for n in range(DETOURS[side][k]):
                relay(side, k, n).wait_send()

    @each_pair
    def _(p):
        for i in range(6):
            wait_send(kv_copy, kv_routes, i, p)
        for i in range(4):
            wait_send(t_copy, t_routes, i, p)

    @each_pair
    def _(p):
        for i in range(2, 6):
            wait_recv(t_copy, t_routes, i, p)
        total = tout[OWN, p].astype(jnp.float32)
        for i in range(2, 6):
            total = total + tin[i, p].astype(jnp.float32)
        dk[:, columns(p)] = total[0].astype(jnp.bfloat16)
        dv[:, columns(p)] = total[1].astype(jnp.bfloat16)
        for i in (4, 5):
            wait_send(t_copy, t_routes, i, p)


def hand_over(*refs):
    sem = refs[-1]
    half = (len(refs) - 1) // 2
    copies = [pltpu.make_async_copy(refs[i], refs[half + i], sem.at[i]) for i in range(half)]
    for copy in copies:
        copy.start()
    for copy in copies:
        copy.wait()


def shards(queries, keys, values, cotangent, partners, counts):
    block = jax.ShapeDtypeStruct((TOK, WIDTH), jnp.bfloat16)
    whole = pl.BlockSpec(memory_space=pl.ANY)
    near = pl.BlockSpec(memory_space=pltpu.VMEM)
    low = jnp.bfloat16
    results = pl.pallas_call(
        kernel,
        out_shape=(pltpu.VMEM((TOK, WIDTH), low),) * 4,
        in_specs=[whole] * 6,
        out_specs=(near,) * 4,
        scratch_shapes=[
            pltpu.VMEM((FRAMES, PAIRS, 2, TOK, PAIR), low),
            pltpu.VMEM((FRAMES, PAIRS, 2, TOK, PAIR), low),
            pltpu.VMEM((6, PAIRS, 2, TOK, PAIR), low),
            pltpu.VMEM((PAIRS, FRAMES, TOK, 2 * TOK), low),
            pltpu.VMEM((PAIRS, TOK, PAIR), low),
            pltpu.VMEM((PAIRS, TOK, PAIR), low),
            pltpu.VMEM((PAIRS, 2 * TOK, PAIR), low),
            pltpu.VMEM((PAIRS, 2, PAIR, TOK), low),
            pltpu.VMEM((PAIRS, 2 * TOK, PAIR), low),
            pltpu.VMEM((PAIRS, 2, PAIR, TOK), low),
            pltpu.VMEM((PAIRS, PAIR, TOK), jnp.float32),
            pltpu.VMEM((PAIRS, FRAMES + 1, 1, 2 * TOK), jnp.float32),
            pltpu.VMEM((PAIRS, 1, 2 * TOK), jnp.float32),
            pltpu.SMEM((FRAMES,), jnp.float32),
            pltpu.SMEM((1, SLOTS), jnp.int32),
            pltpu.SMEM((1, 1), jnp.int32),
            pltpu.SemaphoreType.DMA((2,)),
            pltpu.SemaphoreType.DMA((4, PAIRS)),
            pltpu.SemaphoreType.DMA((6, PAIRS)),
            pltpu.SemaphoreType.DMA((6, PAIRS)),
            pltpu.SemaphoreType.DMA((6, PAIRS)),
            pltpu.SemaphoreType.DMA((6, PAIRS)),
            pltpu.VMEM((len(SEAMS), MOST, 2, TOK, PAIR), low),
            pltpu.SemaphoreType.DMA((len(SEAMS), MOST)),
            pltpu.SemaphoreType.DMA((len(SEAMS), MOST)),
            pltpu.SemaphoreType.REGULAR,
            pltpu.SemaphoreType.REGULAR,
            pltpu.SemaphoreType.REGULAR,
        ],
        compiler_params=pltpu.CompilerParams(
            collective_id=0, has_side_effects=True, vmem_limit_bytes=48 * 2**20
        ),
    )(
        pltpu.with_memory_space_constraint(partners, pltpu.HBM),
        counts.reshape(1, 1),
        *[pltpu.with_memory_space_constraint(x, pltpu.HBM) for x in (queries, keys, values, cotangent)],
    )
    return pl.pallas_call(
        hand_over,
        out_shape=(block,) * 4,
        in_specs=[near] * 4,
        out_specs=(whole,) * 4,
        scratch_shapes=[pltpu.SemaphoreType.DMA((4,))],
    )(*[pltpu.with_memory_space_constraint(x, pltpu.VMEM) for x in results])


def solution(mesh):
    rows = P(("clip", "frame"), None)
    return jax.shard_map(
        shards,
        mesh=mesh,
        in_specs=(rows, rows, rows, rows, rows, P(("clip", "frame"))),
        out_specs=(rows, rows, rows, rows),
        check_vma=False,
    )
```
